512 devices in a mesh: ctx: 128 (over y, z, core), head: 4 (over x).
Axes of the slice: x: 4, y: 8, z: 8, core: 2. Of those that a mesh axis runs over, the one named last changes fastest.
Arguments:
- queries: bfloat16 [16384, 64, 576], P('ctx', 'head'), may hold values from -18 to 18
- latent: bfloat16 [16384, 576], P('ctx'), may hold values from -4 to 4
- out_grad: bfloat16 [16384, 64, 512], P('ctx', 'head'), may hold values from -4 to 4
- doc_blocks: int32 [64], replicated, may hold values from 1 to 4, as said below
Outputs:
- latent_grad: float32 [16384, 576], P('ctx')
The draws below stay inside these ranges and needn't reach their ends.
Inputs may be any that keep to these rules, and one draw needn't show every extreme that they name: `doc_blocks`: they sum to 128; the longest document has exactly 4 blocks.
All inputs are finite; a program needn't handle non-finite values.
Results may differ from the reference program's by a relative error of at most 0.007.
Values may be sent and summed in bfloat16 or wider, within the bound.
No kernel may reach another device: no remote copies, remote signals or barrier semaphores. Data moves between devices by JAX's collectives and lax.ppermute only.
A program may use at most 64 MiB of HBM per device.

```python
import jax
import jax.numpy as jnp
from jax import lax

LAT = 512
ROPE = 64
TOK_DEV = 128
BLOCK = 128
BACK = 3
HEADS = 64
SEQ = 16384
NBLK = 128
NDOC = 64
MOST = 4
N_CTX = 128


def draw_latent(key, part):
    key = jax.random.fold_in(key, 5)
    values = jnp.clip(jax.random.normal(key, (SEQ, LAT + ROPE), jnp.float32), -4.0, 4.0)
    return values.astype(jnp.bfloat16)


def draw_queries(key, part):
    key = jax.random.fold_in(key, 7)
    values = jnp.clip(jax.random.normal(key, (SEQ, HEADS, LAT + ROPE), jnp.float32), -4.0, 4.0)
    return values.astype(jnp.bfloat16)


def draw_doc_blocks(key, part):
    key = jax.random.fold_in(key, 11)
    spread_key, place_key = jax.random.split(key)
    others = NDOC - 1
    slots = others * (MOST - 1)
    extra = NBLK - MOST - others
    order = jax.random.permutation(spread_key, slots)
    taken = (order < extra).astype(jnp.int32).reshape(others, MOST - 1)
    lengths = 1 + jnp.sum(taken, axis=1).astype(jnp.int32)
    joined = jnp.concatenate([lengths, jnp.full((1,), MOST, jnp.int32)]).astype(jnp.int32)
    placing = jax.random.permutation(place_key, NDOC)
    return joined[placing].astype(jnp.int32)


def block_levels(own_key, dims, cuts, low, largest):
    def one(dim, blocks):
        draws = jax.random.uniform(jax.random.fold_in(jax.random.fold_in(own_key, 6), dim), (blocks,), jnp.float32, low / len(cuts), largest / len(cuts))
        return jnp.repeat(jnp.exp(draws), dims[dim] // blocks).reshape((-1,) + (1,) * (len(dims) - dim - 1))

    level = one(*cuts[0])
    for cut in cuts[1:]:
        level = level * one(*cut)
    return level


def noise(rng, extent, scale, bound, pieces=(), held_as=jnp.bfloat16):
    entries = jax.random.normal(rng, extent, jnp.float32) * scale
    if len(pieces) > 0:
        entries = block_levels(rng, extent, pieces, -0.22, 0.18) * entries
    return jnp.clip(entries, min=-bound, max=bound).astype(held_as)


def setup_inputs(seed: int = 0) -> dict:
    seeds = jax.random.split(jax.random.key(seed), 5)
    queries = draw_queries(jax.random.fold_in(seeds[4], 71), 0)
    latent = draw_latent(jax.random.fold_in(seeds[4], 71), 0)
    out_grad = noise(seeds[2], (SEQ, HEADS, LAT), 0.25, 4.0, ((0, 128), (1, 4)))
    doc_blocks = draw_doc_blocks(jax.random.fold_in(seeds[4], 71), 0)
    return dict(queries=queries, latent=latent, out_grad=out_grad, doc_blocks=doc_blocks)


softmax_scale = 192.0 ** -0.5


def doc_index(position, starts):
    return jnp.sum((position[:, None] >= starts[None, :]).astype(jnp.int32), axis=1).astype(jnp.int32)


def window_grads(query_rows, grad_rows, window, visible):
    lat_width = grad_rows.shape[-1]
    query_f = query_rows.astype(jnp.float32)
    grad_f = grad_rows.astype(jnp.float32)
    window_f = window.astype(jnp.float32)
    scores = jnp.einsum("thc,uc->htu", query_f, window_f) * softmax_scale
    scores = jnp.where(visible[None], scores, -jnp.inf)
    row_max = jnp.max(scores, axis=-1, keepdims=True)
    raised = jnp.exp(scores - row_max)
    attn_probs = raised / jnp.sum(raised, axis=-1, keepdims=True)
    probs_low = attn_probs.astype(jnp.bfloat16)
    grad_probs = jnp.einsum("thc,uc->htu", grad_f, window_f[:, :lat_width])
    row_dot = jnp.sum(attn_probs * grad_probs, axis=-1, keepdims=True)
    grad_scores = (attn_probs * (grad_probs - row_dot) * softmax_scale).astype(jnp.bfloat16)
    value_part = jnp.einsum("htu,thc->uc", probs_low.astype(jnp.float32), grad_f)
    key_part = jnp.einsum("htu,thc->uc", grad_scores.astype(jnp.float32), query_f)
    return jnp.concatenate([key_part[:, :lat_width] + value_part, key_part[:, lat_width:]], axis=1)


def reference(queries, latent, out_grad, doc_blocks):
    tok_rows = TOK_DEV
    span = (BACK + 1) * tok_rows
    key_width = latent.shape[1]
    starts = ((jnp.cumsum(doc_blocks) - doc_blocks) * BLOCK).astype(jnp.int32)
    padded = jnp.concatenate([jnp.zeros((BACK * tok_rows, key_width), latent.dtype), latent], axis=0)
    offsets = jnp.arange(tok_rows, dtype=jnp.int32)
    span_offsets = jnp.arange(span, dtype=jnp.int32)

    def one_shard(shard):
        first_row = (shard * tok_rows).astype(jnp.int32)
        query_rows = lax.dynamic_slice_in_dim(queries, first_row, tok_rows, 0)
        grad_rows = lax.dynamic_slice_in_dim(out_grad, first_row, tok_rows, 0)
        window = lax.dynamic_slice_in_dim(padded, first_row, span, 0)
        query_pos = first_row + offsets
        key_pos = first_row - BACK * tok_rows + span_offsets
        same_doc = doc_index(query_pos, starts)[:, None] == doc_index(key_pos, starts)[None, :]
        visible = same_doc & (key_pos[None, :] <= query_pos[:, None])
        return window_grads(query_rows, grad_rows, window, visible)

    shard_grads = lax.map(one_shard, jnp.arange(N_CTX, dtype=jnp.int32))
    shard_grads = shard_grads.reshape(N_CTX, BACK + 1, tok_rows, key_width)
    summed = jnp.zeros(((N_CTX + BACK) * tok_rows, key_width), jnp.float32)
    for offset in range(BACK + 1):
        lower = offset * tok_rows
        summed = summed.at[lower:lower + N_CTX * tok_rows].add(shard_grads[:, offset].reshape(N_CTX * tok_rows, key_width))
    return summed[BACK * tok_rows:]
```

```python
import jax
import jax.numpy as jnp
from jax import lax
from jax.experimental import pallas as pl
from jax.experimental.pallas import tpu as pltpu
from jax.sharding import PartitionSpec as P

BLOCK = 128
BACK = 3
GROUP = 4

softmax_scale = 192.0 ** (-0.5)


def passed_along(x, axis, by):
    peers = lax.axis_size(axis)
    pairs = [(i, i + by) for i in range(peers) if 0 <= i + by < peers]
    return lax.ppermute(x, axis, pairs)


def blocks_back(doc_blocks, block):
    count = doc_blocks.shape[0]
    earlier = jnp.arange(count)[:, None] > jnp.arange(count)[None, :]
    starts = jnp.sum(jnp.where(earlier, doc_blocks[None, :], 0), axis=1)
    first = jnp.max(jnp.where(starts <= block, starts, 0))
    return (block - first).astype(jnp.int32).reshape(1)


def grads_kernel(back_ref, q_ref, g_ref, k3_ref, k2_ref, k1_ref, k0_ref, far_ref, own_ref, keys, total):
    step = pl.program_id(0)
    span, width = keys.shape
    lat = g_ref.shape[1]
    blk = k0_ref.shape[1]

    @pl.when(step == 0)
    def _():
        for j, ref in enumerate((k3_ref, k2_ref, k1_ref, k0_ref)):
            keys[j * blk:(j + 1) * blk, :] = ref[...].T

    q = jnp.concatenate([q_ref[h] for h in range(GROUP)], axis=1)
    g = jnp.concatenate([g_ref[h] for h in range(GROUP)], axis=1)
    cols = q.shape[1]
    window = keys[...]
    scores = jnp.dot(window, q, preferred_element_type=jnp.float32) * softmax_scale
    grad_probs = jnp.dot(window[:, :lat], g, preferred_element_type=jnp.float32)
    row = lax.broadcasted_iota(jnp.int32, (span, cols), 0)
    col = lax.broadcasted_iota(jnp.int32, (span, cols), 1)
    first = (BACK - back_ref[0]) * blk
    visible = (row >= first) & (row <= BACK * blk + (col & (blk - 1)))
    scores = jnp.where(visible, scores, -jnp.inf)
    raised = jnp.exp(scores - jnp.max(scores, axis=0, keepdims=True))
    probs = raised * (1.0 / jnp.sum(raised, axis=0, keepdims=True))
    dot = jnp.sum(probs * grad_probs, axis=0, keepdims=True)
    grad_scores = (probs * (grad_probs - dot) * softmax_scale).astype(jnp.bfloat16)
    low = probs.astype(jnp.bfloat16)
    nt = (((1,), (1,)), ((), ()))
    upper = lax.dot_general(
        jnp.concatenate([q[:lat], g], axis=1),
        jnp.concatenate([grad_scores, low], axis=1),
        nt, preferred_element_type=jnp.float32)
    lower = lax.dot_general(q[lat:], grad_scores, nt, preferred_element_type=jnp.float32)

    @pl.when(step == 0)
    def _():
        total[:lat, :] = upper
        total[lat:, :] = lower

    @pl.when(step > 0)
    def _():
        total[:lat, :] += upper
        total[lat:, :] += lower

    @pl.when(step == pl.num_programs(0) - 1)
    def _():
        for j in range(BACK):
            far_ref[j] = total[:, j * blk:(j + 1) * blk].astype(far_ref.dtype)
        own_ref[...] = total[:, BACK * blk:]


def window_grads(back, q, g, keys):
    heads, width, rows = q.shape
    lat = g.shape[1]
    whole = pl.BlockSpec((width, rows), lambda i: (0, 0))
    return pl.pallas_call(
        grads_kernel,
        grid=(heads // GROUP,),
        in_specs=[
            pl.BlockSpec(memory_space=pltpu.SMEM),
            pl.BlockSpec((GROUP, width, rows), lambda i: (i, 0, 0)),
            pl.BlockSpec((GROUP, lat, rows), lambda i: (i, 0, 0)),
            whole, whole, whole, whole,
        ],
        out_specs=[pl.BlockSpec((BACK, width, rows), lambda i: (0, 0, 0)), whole],
        out_shape=[
            jax.ShapeDtypeStruct((BACK, width, rows), jnp.bfloat16),
            jax.ShapeDtypeStruct((width, rows), jnp.float32),
        ],
        scratch_shapes=[
            pltpu.VMEM(((BACK + 1) * rows, width), jnp.bfloat16),
            pltpu.VMEM((width, (BACK + 1) * rows), jnp.float32),
        ],
        compiler_params=pltpu.CompilerParams(vmem_limit_bytes=40 * 1024 * 1024),
        name="window_grads",
    )(back, q, g, *keys)


def shards(queries, latent, out_grad, doc_blocks):
    own = latent.T
    keys = [passed_along(own, "ctx", offset) for offset in range(BACK, 0, -1)] + [own]
    back = blocks_back(doc_blocks, lax.axis_index("ctx"))
    q = jnp.transpose(queries, (1, 2, 0))
    g = jnp.transpose(out_grad, (1, 2, 0))
    far, near = window_grads(back, q, g, keys)
    for offset in range(BACK, 0, -1):
        near = near + passed_along(far[BACK - offset], "ctx", -offset).astype(jnp.float32)
    low = near.astype(jnp.bfloat16)
    heads = lax.axis_size("head")
    spread = jnp.broadcast_to(low[None], (heads,) + low.shape)
    parts = lax.all_to_all(spread, "head", 0, 0, tiled=True)
    return jnp.sum(parts.astype(jnp.float32), axis=0).T


def solution(mesh):
    return jax.shard_map(
        shards,
        mesh=mesh,
        in_specs=(P("ctx", "head", None), P("ctx", None), P("ctx", "head", None), P()),
        out_specs=P("ctx", None),
        check_vma=False,
    )
```

```python
import math

import jax
import jax.numpy as jnp
from jax import lax
from jax.experimental import pallas as pl
from jax.experimental.pallas import tpu as pltpu
from jax.sharding import PartitionSpec as P

BLOCK = 128
GROUP = 8
LANES = 128
OWN_FLOPS = 4 * 10 ** 9

softmax_scale = 192.0 ** (-0.5)
to_exponent = softmax_scale * math.log2(math.e)
NT = (((1,), (1,)), ((), ()))
VMEM = pl.BlockSpec(memory_space=pltpu.VMEM)
SMEM = pl.BlockSpec(memory_space=pltpu.SMEM)


def skip_pairs(n):
    ahead = [(i, i + 1 if i % 2 == 0 else i + 3) for i in range(n)]
    return [(i, j) for i, j in ahead if j < n]


def step_pairs(n):
    return [(i, i + 2) for i in range(n - 2)]


def swap_pairs(n):
    return [(i, i ^ 1) for i in range(n)]


def turned(pairs):
    return [(j, i) for i, j in pairs]


def side_by_side(ref, at):
    return jnp.concatenate([ref[at + h] for h in range(GROUP)], axis=1)


def own_kernel(shard_ref, docs_ref, g_ref, own_ref, seen_ref, grads_ref):
    heads, lat, blk = g_ref.shape

    docs = docs_ref[...]
    square = (docs.shape[1], docs.shape[1])
    earlier = lax.broadcasted_iota(jnp.int32, square, 1) < lax.broadcasted_iota(jnp.int32, square, 0)
    starts = jnp.sum(jnp.where(earlier, docs, 0), axis=1, keepdims=True)
    shard = shard_ref[0]
    first = jnp.max(jnp.where(starts <= shard, starts, 0), axis=0, keepdims=True)
    even = lax.rem(shard, 2) == 0
    slot = lax.broadcasted_iota(jnp.int32, seen_ref.shape, 0)
    offset = jnp.where(slot == 0, jnp.where(even, 1, 3), jnp.where(slot == 1, jnp.where(even, 3, 1), 2))
    seen_ref[...] = (offset <= shard - first).astype(jnp.int32)

    rows = own_ref[:lat, :].T
    for at in range(0, heads, GROUP):
        grads_ref[:, at * blk:(at + GROUP) * blk] = jnp.dot(
            rows, side_by_side(g_ref, at), preferred_element_type=jnp.float32)


def own_grads(shard, doc_blocks, g, own):
    heads, lat, rows = g.shape
    return pl.pallas_call(
        own_kernel,
        in_specs=[SMEM] + [VMEM] * 3, out_specs=[VMEM, VMEM],
        out_shape=[
            jax.ShapeDtypeStruct((8, LANES), jnp.int32),
            jax.ShapeDtypeStruct((rows, heads * rows), jnp.float32),
        ],
        compiler_params=pltpu.CompilerParams(vmem_limit_bytes=30 * 1024 * 1024),
        cost_estimate=pl.CostEstimate(flops=OWN_FLOPS, bytes_accessed=0, transcendentals=0),
        name="own_grads",
    )(shard, doc_blocks, g, own)


def products_kernel(q_ref, g_ref, step_ref, own_ref, scores_ref, grads_ref):
    heads, lat, blk = g_ref.shape
    rows = jnp.concatenate([step_ref[...].T, own_ref[...].T], axis=0)
    for at in range(0, heads, GROUP):
        where = slice(at * blk, (at + GROUP) * blk)
        scores = jnp.dot(rows, side_by_side(q_ref, at), preferred_element_type=jnp.float32)
        key = lax.broadcasted_iota(jnp.int32, scores[blk:].shape, 0)
        query = lax.broadcasted_iota(jnp.int32, scores[blk:].shape, 1) & (blk - 1)
        scores_ref[:blk, where] = scores[:blk]
        scores_ref[blk:, where] = jnp.where(key <= query, scores[blk:], -jnp.inf)
        grads_ref[:, where] = jnp.dot(
            rows[:blk, :lat], side_by_side(g_ref, at), preferred_element_type=jnp.float32)


def products(q, g, step, own):
    heads, width, rows = q.shape
    return pl.pallas_call(
        products_kernel,
        in_specs=[VMEM] * 4, out_specs=[VMEM, VMEM],
        out_shape=[
            jax.ShapeDtypeStruct((2 * rows, heads * rows), jnp.float32),
            jax.ShapeDtypeStruct((rows, heads * rows), jnp.float32),
        ],
        compiler_params=pltpu.CompilerParams(vmem_limit_bytes=30 * 1024 * 1024),
        name="products",
    )(q, g, step, own)


def transposed_sums(q, g, grad_scores, low):
    lat = g.shape[0]
    upper = lax.dot_general(
        jnp.concatenate([q[:lat], g], axis=1), jnp.concatenate([grad_scores, low], axis=1),
        NT, preferred_element_type=jnp.float32)
    lower = lax.dot_general(q[lat:], grad_scores, NT, preferred_element_type=jnp.float32)
    return upper, lower


def put(refs, upper, lower):
    lat = upper.shape[0]
    for j, ref in enumerate(refs):
        blk = ref.shape[1]
        ref[:lat, :] = upper[:, j * blk:(j + 1) * blk].astype(ref.dtype)
        ref[lat:, :] = lower[:, j * blk:(j + 1) * blk].astype(ref.dtype)


def first_kernel(seen_ref, q_ref, g_ref, swap_ref, skip_ref, near_s, step_g, own_g,
                 swap_out, skip_out, scores_out, low_out):
    heads, lat, blk = g_ref.shape
    rows = jnp.concatenate([swap_ref[...].T, skip_ref[...].T], axis=0)
    upper = lower = None
    for at in range(0, heads, GROUP):
        where = pl.ds(at * blk, GROUP * blk)
        q = side_by_side(q_ref, at)
        g = side_by_side(g_ref, at)
        scores = jnp.dot(rows, q, preferred_element_type=jnp.float32)
        grad_probs = jnp.dot(rows[:, :lat], g, preferred_element_type=jnp.float32)
        grad_probs = jnp.concatenate([grad_probs, step_g[:, where], own_g[:, where]], axis=0)
        parts = [scores[:blk], scores[blk:], near_s[:blk, where], near_s[blk:, where]]
        tops = [jnp.max(part, axis=0, keepdims=True) for part in parts]
        top = tops[3]
        for j in range(3):
            top = jnp.maximum(top, jnp.where(seen_ref[j:j + 1, :1] > 0, tops[j], -jnp.inf))
        top = top * to_exponent
        less = [jnp.where(seen_ref[j:j + 1, :1] > 0, top, jnp.inf) for j in range(3)] + [top]
        raised = jnp.concatenate([jnp.exp2(p * to_exponent - b) for p, b in zip(parts, less)], axis=0)
        inverse = 1.0 / jnp.sum(raised, axis=0, keepdims=True)
        dot = jnp.sum(raised * grad_probs, axis=0, keepdims=True) * inverse
        low = (raised * inverse).astype(jnp.bfloat16)
        grad_scores = ((raised * (inverse * softmax_scale)) * (grad_probs - dot)).astype(jnp.bfloat16)
        scores_out[:, where] = grad_scores[2 * blk:]
        low_out[:, where] = low[2 * blk:]
        up, down = transposed_sums(q, g, grad_scores[:2 * blk], low[:2 * blk])
        upper = up if upper is None else upper + up
        lower = down if lower is None else lower + down
    put((swap_out, skip_out), upper, lower)


def first_grads(seen, q, g, swap, skip, near_scores, step_grads, own_grads):
    heads, width, rows = q.shape
    sent = jax.ShapeDtypeStruct((width, rows), jnp.bfloat16)
    kept = jax.ShapeDtypeStruct((2 * rows, heads * rows), jnp.bfloat16)
    return pl.pallas_call(
        first_kernel,
        in_specs=[VMEM] * 8, out_specs=[VMEM] * 4, out_shape=[sent, sent, kept, kept],
        compiler_params=pltpu.CompilerParams(vmem_limit_bytes=30 * 1024 * 1024),
        name="first_grads",
    )(seen, q, g, swap, skip, near_scores, step_grads, own_grads)


def second_kernel(q_ref, g_ref, scores_ref, low_ref, step_out, own_out):
    heads, lat, blk = g_ref.shape
    upper = lower = None
    for at in range(0, heads, GROUP):
        where = pl.ds(at * blk, GROUP * blk)
        up, down = transposed_sums(
            side_by_side(q_ref, at), side_by_side(g_ref, at), scores_ref[:, where], low_ref[:, where])
        upper = up if upper is None else upper + up
        lower = down if lower is None else lower + down
    put((step_out, own_out), upper, lower)


def second_grads(q, g, grad_scores, low):
    heads, width, rows = q.shape
    made = jax.ShapeDtypeStruct((width, rows), jnp.float32)
    return pl.pallas_call(
        second_kernel,
        in_specs=[VMEM] * 4, out_specs=[VMEM] * 2, out_shape=[made, made],
        compiler_params=pltpu.CompilerParams(vmem_limit_bytes=30 * 1024 * 1024),
        name="second_grads",
    )(q, g, grad_scores, low)


def after(x, *others):
    return lax.optimization_barrier((x,) + others)[0]


def shards(queries, latent, out_grad, doc_blocks):
    n = lax.axis_size("ctx")
    shard = lax.axis_index("ctx")
    own = latent.T
    step = lax.ppermute(own, "ctx", step_pairs(n))
    skip = lax.ppermute(own, "ctx", skip_pairs(n))
    q = jnp.transpose(queries, (1, 2, 0))
    g = jnp.transpose(out_grad, (1, 2, 0))
    seen, of_own = own_grads(shard.reshape(1), doc_blocks.reshape(1, -1), g, own)
    step = after(step, of_own)
    swap = lax.ppermute(step, "ctx", swap_pairs(n))
    near_scores, of_step = products(q, g, step, own)
    swap, skip, grad_scores, low = first_grads(seen, q, g, swap, skip, near_scores, of_step, of_own)
    swap = lax.ppermute(swap, "ctx", swap_pairs(n))
    skip = lax.ppermute(skip, "ctx", turned(skip_pairs(n)))
    step, near = second_grads(q, g, grad_scores, low)
    step = (step + swap.astype(jnp.float32)).astype(jnp.bfloat16)
    step = lax.ppermute(step, "ctx", turned(step_pairs(n)))
    low = (near + skip.astype(jnp.float32) + step.astype(jnp.float32)).astype(jnp.bfloat16)
    heads = lax.axis_size("head")
    spread = jnp.broadcast_to(low[None], (heads,) + low.shape)
    parts = lax.all_to_all(spread, "head", 0, 0, tiled=True)
    return jnp.sum(parts.astype(jnp.float32), axis=0).T


def solution(mesh):
    return jax.shard_map(
        shards,
        mesh=mesh,
        in_specs=(P("ctx", "head", None), P("ctx", None), P("ctx", "head", None), P()),
        out_specs=P("ctx", None),
        check_vma=False,
    )
```

```python
import math

import jax
import jax.numpy as jnp
from jax import lax
from jax.experimental import pallas as pl
from jax.experimental.pallas import tpu as pltpu
from jax.sharding import PartitionSpec as P

BLOCK = 128
GROUP = 8
PART = 4
LANES = 128
OWN_FLOPS = 1 * 10 ** 9

softmax_scale = 192.0 ** (-0.5)
to_exponent = softmax_scale * math.log2(math.e)
NT = (((1,), (1,)), ((), ()))
VMEM = pl.BlockSpec(memory_space=pltpu.VMEM)
SMEM = pl.BlockSpec(memory_space=pltpu.SMEM)


def skip_pairs(n):
    ahead = [(i, i + 1 if i % 2 == 0 else i + 3) for i in range(n)]
    return [(i, j) for i, j in ahead if j < n]


def step_pairs(n):
    return [(i, i + 2) for i in range(n - 2)]


def swap_pairs(n):
    return [(i, i ^ 1) for i in range(n)]


def turned(pairs):
    return [(j, i) for i, j in pairs]


def side_by_side(ref, at, count):
    return jnp.concatenate([ref[at + h] for h in range(count)], axis=1)


def own_kernel(shard_ref, docs_ref, g_ref, own_ref, seen_ref, grads_ref):
    heads, lat, blk = g_ref.shape

    docs = docs_ref[...]
    square = (docs.shape[1], docs.shape[1])
    earlier = lax.broadcasted_iota(jnp.int32, square, 1) < lax.broadcasted_iota(jnp.int32, square, 0)
    starts = jnp.sum(jnp.where(earlier, docs, 0), axis=1, keepdims=True)
    shard = shard_ref[0]
    first = jnp.max(jnp.where(starts <= shard, starts, 0), axis=0, keepdims=True)
    even = lax.rem(shard, 2) == 0
    slot = lax.broadcasted_iota(jnp.int32, seen_ref.shape, 0)
    offset = jnp.where(slot == 0, jnp.where(even, 1, 3), jnp.where(slot == 1, jnp.where(even, 3, 1), 2))
    seen_ref[...] = (offset <= shard - first).astype(jnp.int32)

    rows = own_ref[:lat, :].T
    for at in range(0, heads, GROUP):
        grads_ref[:, at * blk:(at + GROUP) * blk] = jnp.dot(
            rows, side_by_side(g_ref, at, GROUP), preferred_element_type=jnp.float32)


def own_grads(shard, doc_blocks, g, own):
    heads, lat, rows = g.shape
    return pl.pallas_call(
        own_kernel,
        in_specs=[SMEM] + [VMEM] * 3, out_specs=[VMEM, VMEM],
        out_shape=[
            jax.ShapeDtypeStruct((8, LANES), jnp.int32),
            jax.ShapeDtypeStruct((rows, heads * rows), jnp.float32),
        ],
        compiler_params=pltpu.CompilerParams(vmem_limit_bytes=30 * 1024 * 1024),
        cost_estimate=pl.CostEstimate(flops=OWN_FLOPS, bytes_accessed=0, transcendentals=0),
        name="own_grads",
    )(shard, doc_blocks, g, own)


def products_kernel(q_ref, g_ref, step_ref, own_ref, scores_ref, grads_ref):
    heads, lat, blk = g_ref.shape
    rows = jnp.concatenate([step_ref[...].T, own_ref[...].T], axis=0)
    for at in range(0, heads, GROUP):
        where = slice(at * blk, (at + GROUP) * blk)
        scores = jnp.dot(rows, side_by_side(q_ref, at, GROUP), preferred_element_type=jnp.float32)
        key = lax.broadcasted_iota(jnp.int32, scores[blk:].shape, 0)
        query = lax.broadcasted_iota(jnp.int32, scores[blk:].shape, 1) & (blk - 1)
        scores_ref[:blk, where] = scores[:blk]
        scores_ref[blk:, where] = jnp.where(key <= query, scores[blk:], -jnp.inf)
        grads_ref[:, where] = jnp.dot(
            rows[:blk, :lat], side_by_side(g_ref, at, GROUP), preferred_element_type=jnp.float32)


def products(q, g, step, own):
    heads, width, rows = q.shape
    return pl.pallas_call(
        products_kernel,
        in_specs=[VMEM] * 4, out_specs=[VMEM, VMEM],
        out_shape=[
            jax.ShapeDtypeStruct((2 * rows, heads * rows), jnp.float32),
            jax.ShapeDtypeStruct((rows, heads * rows), jnp.float32),
        ],
        compiler_params=pltpu.CompilerParams(vmem_limit_bytes=30 * 1024 * 1024),
        name="products",
    )(q, g, step, own)


def first_kernel(seen_ref, q_ref, g_ref, swap_ref, skip_ref, near_s, step_g, own_g,
                 swap_out, skip_out, step_out, own_out):
    heads, lat, blk = g_ref.shape
    rows = jnp.concatenate([swap_ref[...].T, skip_ref[...].T], axis=0)

    def products_of(at):
        q = side_by_side(q_ref, at, PART)
        g = side_by_side(g_ref, at, PART)
        scores = jnp.dot(rows, q, preferred_element_type=jnp.float32)
        grad_probs = jnp.dot(rows[:, :lat], g, preferred_element_type=jnp.float32)
        return at, q, g, scores, grad_probs

    def sums_of(at, q, g, scores, grad_probs):
        where = slice(at * blk, (at + PART) * blk)
        grad_probs = jnp.concatenate([grad_probs, step_g[:, where], own_g[:, where]], axis=0)
        parts = [scores[:blk], scores[blk:], near_s[:blk, where], near_s[blk:, where]]
        tops = [jnp.max(part, axis=0, keepdims=True) for part in parts]
        top = tops[3]
        for j in range(3):
            top = jnp.maximum(top, jnp.where(seen_ref[j:j + 1, :1] > 0, tops[j], -jnp.inf))
        top = top * to_exponent
        less = [jnp.where(seen_ref[j:j + 1, :1] > 0, top, jnp.inf) for j in range(3)] + [top]
        raised = jnp.concatenate([jnp.exp2(p * to_exponent - b) for p, b in zip(parts, less)], axis=0)
        inverse = 1.0 / jnp.sum(raised, axis=0, keepdims=True)
        dot = jnp.sum(raised * grad_probs, axis=0, keepdims=True) * inverse
        low = (raised * inverse).astype(jnp.bfloat16)
        grad_scores = ((raised * (inverse * softmax_scale)) * (grad_probs - dot)).astype(jnp.bfloat16)
        value = lax.dot_general(g, low, NT, preferred_element_type=jnp.float32)
        key = lax.dot_general(q, grad_scores, NT, preferred_element_type=jnp.float32)
        return value, key

    value = key = None
    after_this = products_of(0)
    for at in range(0, heads, PART):
        this = after_this
        if at + PART < heads:
            after_this = products_of(at + PART)
        more_value, more_key = sums_of(*this)
        value = more_value if value is None else value + more_value
        key = more_key if key is None else key + more_key
    for j, ref in enumerate((swap_out, skip_out, step_out, own_out)):
        mine = slice(j * blk, (j + 1) * blk)
        ref[:lat, :] = (key[:lat, mine] + value[:, mine]).astype(ref.dtype)
        ref[lat:, :] = key[lat:, mine].astype(ref.dtype)


def first_grads(seen, q, g, swap, skip, near_scores, step_grads, own_grads):
    heads, width, rows = q.shape
    sent = jax.ShapeDtypeStruct((width, rows), jnp.bfloat16)
    kept = jax.ShapeDtypeStruct((width, rows), jnp.float32)
    return pl.pallas_call(
        first_kernel,
        in_specs=[VMEM] * 8, out_specs=[VMEM] * 4, out_shape=[sent, sent, kept, kept],
        compiler_params=pltpu.CompilerParams(vmem_limit_bytes=30 * 1024 * 1024),
        name="first_grads",
    )(seen, q, g, swap, skip, near_scores, step_grads, own_grads)


def after(x, *others):
    return lax.optimization_barrier((x,) + others)[0]


def shards(queries, latent, out_grad, doc_blocks):
    n = lax.axis_size("ctx")
    shard = lax.axis_index("ctx")
    own = latent.T
    step = lax.ppermute(own, "ctx", step_pairs(n))
    skip = lax.ppermute(own, "ctx", skip_pairs(n))
    q = jnp.transpose(queries, (1, 2, 0))
    g = jnp.transpose(out_grad, (1, 2, 0))
    seen, of_own = own_grads(shard.reshape(1), doc_blocks.reshape(1, -1), g, own)
    step = after(step, of_own)
    swap = lax.ppermute(step, "ctx", swap_pairs(n))
    near_scores, of_step = products(q, g, step, own)
    swap, skip, step, near = first_grads(seen, q, g, swap, skip, near_scores, of_step, of_own)
    swap = lax.ppermute(swap, "ctx", swap_pairs(n))
    skip = lax.ppermute(skip, "ctx", turned(skip_pairs(n)))
    step = (step + swap.astype(jnp.float32)).astype(jnp.bfloat16)
    step = lax.ppermute(step, "ctx", turned(step_pairs(n)))
    low = (near + skip.astype(jnp.float32) + step.astype(jnp.float32)).astype(jnp.bfloat16)
    heads = lax.axis_size("head")
    spread = jnp.broadcast_to(low[None], (heads,) + low.shape)
    parts = lax.all_to_all(spread, "head", 0, 0, tiled=True)
    return jnp.sum(parts.astype(jnp.float32), axis=0).T


def solution(mesh):
    return jax.shard_map(
        shards,
        mesh=mesh,
        in_specs=(P("ctx", "head", None), P("ctx", None), P("ctx", "head", None), P()),
        out_specs=P("ctx", None),
        check_vma=False,
    )
```

```python
import math

import jax
import jax.numpy as jnp
from jax import lax
from jax.experimental import pallas as pl
from jax.experimental.pallas import tpu as pltpu
from jax.sharding import PartitionSpec as P

BLOCK = 128
GROUP = 8
PART = 4
LANES = 128
OWN_FLOPS = 1 * 10 ** 9

softmax_scale = 192.0 ** (-0.5)
to_exponent = softmax_scale * math.log2(math.e)
NT = (((1,), (1,)), ((), ()))
VMEM = pl.BlockSpec(memory_space=pltpu.VMEM)
SMEM = pl.BlockSpec(memory_space=pltpu.SMEM)


def skip_pairs(n):
    ahead = [(i, i + 1 if i % 2 == 0 else i + 3) for i in range(n)]
    return [(i, j) for i, j in ahead if j < n]


def step_pairs(n):
    return [(i, i + 2) for i in range(n - 2)]


def swap_pairs(n):
    return [(i, i ^ 1) for i in range(n)]


def turned(pairs):
    return [(j, i) for i, j in pairs]


def side_by_side(ref, at, count):
    return jnp.concatenate([ref[at + h] for h in range(count)], axis=1)


def own_kernel(shard_ref, docs_ref, g_ref, own_ref, seen_ref, grads_ref):
    heads, lat, blk = g_ref.shape

    docs = docs_ref[...]
    square = (docs.shape[1], docs.shape[1])
    earlier = lax.broadcasted_iota(jnp.int32, square, 1) < lax.broadcasted_iota(jnp.int32, square, 0)
    starts = jnp.sum(jnp.where(earlier, docs, 0), axis=1, keepdims=True)
    shard = shard_ref[0]
    first = jnp.max(jnp.where(starts <= shard, starts, 0), axis=0, keepdims=True)
    even = lax.rem(shard, 2) == 0
    slot = lax.broadcasted_iota(jnp.int32, seen_ref.shape, 0)
    offset = jnp.where(slot == 0, jnp.where(even, 1, 3), jnp.where(slot == 1, jnp.where(even, 3, 1), 2))
    seen_ref[...] = (offset <= shard - first).astype(jnp.int32)

    rows = own_ref[:lat, :].T
    for at in range(0, heads, GROUP):
        grads_ref[:, at * blk:(at + GROUP) * blk] = jnp.dot(
            rows, side_by_side(g_ref, at, GROUP), preferred_element_type=jnp.float32)


def own_grads(shard, doc_blocks, g, own):
    heads, lat, rows = g.shape
    return pl.pallas_call(
        own_kernel,
        in_specs=[SMEM] + [VMEM] * 3, out_specs=[VMEM, VMEM],
        out_shape=[
            jax.ShapeDtypeStruct((8, LANES), jnp.int32),
            jax.ShapeDtypeStruct((rows, heads * rows), jnp.float32),
        ],
        compiler_params=pltpu.CompilerParams(vmem_limit_bytes=30 * 1024 * 1024),
        cost_estimate=pl.CostEstimate(flops=OWN_FLOPS, bytes_accessed=0, transcendentals=0),
        name="own_grads",
    )(shard, doc_blocks, g, own)


def products_kernel(q_ref, g_ref, step_ref, own_ref, scores_ref, grads_ref):
    heads, lat, blk = g_ref.shape
    rows = jnp.concatenate([step_ref[...].T, own_ref[...].T], axis=0)
    for at in range(0, heads, GROUP):
        where = slice(at * blk, (at + GROUP) * blk)
        scores = jnp.dot(rows, side_by_side(q_ref, at, GROUP), preferred_element_type=jnp.float32)
        key = lax.broadcasted_iota(jnp.int32, scores[blk:].shape, 0)
        query = lax.broadcasted_iota(jnp.int32, scores[blk:].shape, 1) & (blk - 1)
        scores_ref[:blk, where] = scores[:blk]
        scores_ref[blk:, where] = jnp.where(key <= query, scores[blk:], -jnp.inf)
        grads_ref[:, where] = jnp.dot(
            rows[:blk, :lat], side_by_side(g_ref, at, GROUP), preferred_element_type=jnp.float32)


def products(q, g, step, own):
    heads, width, rows = q.shape
    return pl.pallas_call(
        products_kernel,
        in_specs=[VMEM] * 4, out_specs=[VMEM, VMEM],
        out_shape=[
            jax.ShapeDtypeStruct((2 * rows, heads * rows), jnp.float32),
            jax.ShapeDtypeStruct((rows, heads * rows), jnp.float32),
        ],
        compiler_params=pltpu.CompilerParams(vmem_limit_bytes=30 * 1024 * 1024),
        name="products",
    )(q, g, step, own)


def first_kernel(seen_ref, q_ref, g_ref, swap_ref, skip_ref, near_s, step_g, own_g,
                 swap_out, skip_out, step_out, own_out):
    heads, lat, blk = g_ref.shape
    rows = jnp.concatenate([swap_ref[...].T, skip_ref[...].T], axis=0)

    def products_of(at):
        q = side_by_side(q_ref, at, PART)
        g = side_by_side(g_ref, at, PART)
        scores = jnp.dot(rows, q, preferred_element_type=jnp.float32)
        grad_probs = jnp.dot(rows[:, :lat], g, preferred_element_type=jnp.float32)
        return at, q, g, scores, grad_probs

    def sums_of(at, q, g, scores, grad_probs):
        where = slice(at * blk, (at + PART) * blk)
        grad_probs = jnp.concatenate([grad_probs, step_g[:, where], own_g[:, where]], axis=0)
        parts = [scores[:blk], scores[blk:], near_s[:blk, where], near_s[blk:, where]]
        tops = [jnp.max(part, axis=0, keepdims=True) for part in parts]
        top = tops[3]
        for j in range(3):
            top = jnp.maximum(top, jnp.where(seen_ref[j:j + 1, :1] > 0, tops[j], -jnp.inf))
        top = top * to_exponent
        less = [jnp.where(seen_ref[j:j + 1, :1] > 0, top, jnp.inf) for j in range(3)] + [top]
        raised = jnp.concatenate([jnp.exp2(p * to_exponent - b) for p, b in zip(parts, less)], axis=0)
        inverse = 1.0 / jnp.sum(raised, axis=0, keepdims=True)
        dot = jnp.sum(raised * grad_probs, axis=0, keepdims=True) * inverse
        low = (raised * inverse).astype(jnp.bfloat16)
        grad_scores = ((raised * (inverse * softmax_scale)) * (grad_probs - dot)).astype(jnp.bfloat16)
        value = lax.dot_general(g, low, NT, preferred_element_type=jnp.float32)
        key = lax.dot_general(q, grad_scores, NT, preferred_element_type=jnp.float32)
        return value, key

    value = key = None
    after_this = products_of(0)
    for at in range(0, heads, PART):
        this = after_this
        if at + PART < heads:
            after_this = products_of(at + PART)
        more_value, more_key = sums_of(*this)
        value = more_value if value is None else value + more_value
        key = more_key if key is None else key + more_key
    for j, ref in enumerate((swap_out, skip_out, step_out, own_out)):
        mine = slice(j * blk, (j + 1) * blk)
        ref[:lat, :] = (key[:lat, mine] + value[:, mine]).astype(ref.dtype)
        ref[lat:, :] = key[lat:, mine].astype(ref.dtype)


def first_grads(seen, q, g, swap, skip, near_scores, step_grads, own_grads):
    heads, width, rows = q.shape
    sent = jax.ShapeDtypeStruct((width, rows), jnp.bfloat16)
    kept = jax.ShapeDtypeStruct((width, rows), jnp.float32)
    return pl.pallas_call(
        first_kernel,
        in_specs=[VMEM] * 8, out_specs=[VMEM] * 4, out_shape=[sent, sent, kept, kept],
        compiler_params=pltpu.CompilerParams(vmem_limit_bytes=30 * 1024 * 1024),
        name="first_grads",
    )(seen, q, g, swap, skip, near_scores, step_grads, own_grads)


def after(x, *others):
    return lax.optimization_barrier((x,) + others)[0]


def from_partner(x, n, shard):
    both = lax.all_gather(x, "ctx", axis_index_groups=[[i, i + 1] for i in range(0, n, 2)])
    return jnp.where(shard % 2 == 0, both[1], both[0])


def shards(queries, latent, out_grad, doc_blocks):
    n = lax.axis_size("ctx")
    shard = lax.axis_index("ctx")
    own = latent.T
    step = lax.ppermute(own, "ctx", step_pairs(n))
    skip = lax.ppermute(own, "ctx", skip_pairs(n))
    q = jnp.transpose(queries, (1, 2, 0))
    g = jnp.transpose(out_grad, (1, 2, 0))
    seen, of_own = own_grads(shard.reshape(1), doc_blocks.reshape(1, -1), g, own)
    step = after(step, of_own)
    swap = from_partner(step, n, shard)
    near_scores, of_step = products(q, g, step, own)
    swap, skip, step, near = first_grads(seen, q, g, swap, skip, near_scores, of_step, of_own)
    swap = from_partner(swap, n, shard)
    step = (step + swap.astype(jnp.float32)).astype(jnp.bfloat16)
    skip = after(skip, step)
    step = lax.ppermute(step, "ctx", turned(step_pairs(n)))
    skip = lax.ppermute(skip, "ctx", turned(skip_pairs(n)))
    near = near + step.astype(jnp.float32)
    near, skip = lax.optimization_barrier((near, skip))
    low = (near + skip.astype(jnp.float32)).astype(jnp.bfloat16)
    low = jnp.sum(lax.all_gather(low, "head", axis_index_groups=[[0, 1], [2, 3]]).astype(jnp.float32), axis=0)
    parts = lax.all_gather(low.astype(jnp.bfloat16), "head", axis_index_groups=[[0, 3], [1, 2]])
    return jnp.sum(parts.astype(jnp.float32), axis=0).T


def solution(mesh):
    return jax.shard_map(
        shards,
        mesh=mesh,
        in_specs=(P("ctx", "head", None), P("ctx", None), P("ctx", "head", None), P()),
        out_specs=P("ctx", None),
        check_vma=False,
    )
```

```python
import math

import jax
import jax.numpy as jnp
from jax import lax
from jax.experimental import pallas as pl
from jax.experimental.pallas import tpu as pltpu
from jax.sharding import PartitionSpec as P

BLOCK = 128
GROUP = 8
PART = 4
TILE = 16
HEADROOM = 14
FIRST_PAIRS = [[0, 1], [2, 3]]
SECOND_PAIRS = [[0, 3], [1, 2]]
LANES = 128
OWN_FLOPS = 1 * 10 ** 9

softmax_scale = 192.0 ** (-0.5)
to_exponent = softmax_scale * math.log2(math.e)
NT = (((1,), (1,)), ((), ()))
VMEM = pl.BlockSpec(memory_space=pltpu.VMEM)
SMEM = pl.BlockSpec(memory_space=pltpu.SMEM)


def skip_pairs(n):
    ahead = [(i, i + 1 if i % 2 == 0 else i + 3) for i in range(n)]
    return [(i, j) for i, j in ahead if j < n]


def step_pairs(n):
    return [(i, i + 2) for i in range(n - 2)]


def swap_pairs(n):
    return [(i, i ^ 1) for i in range(n)]


def turned(pairs):
    return [(j, i) for i, j in pairs]


def side_by_side(ref, at, count):
    return jnp.concatenate([ref[at + h] for h in range(count)], axis=1)


def own_kernel(shard_ref, docs_ref, g_ref, own_ref, seen_ref, grads_ref):
    heads, lat, blk = g_ref.shape

    docs = docs_ref[...]
    square = (docs.shape[1], docs.shape[1])
    earlier = lax.broadcasted_iota(jnp.int32, square, 1) < lax.broadcasted_iota(jnp.int32, square, 0)
    starts = jnp.sum(jnp.where(earlier, docs, 0), axis=1, keepdims=True)
    shard = shard_ref[0]
    first = jnp.max(jnp.where(starts <= shard, starts, 0), axis=0, keepdims=True)
    even = lax.rem(shard, 2) == 0
    slot = lax.broadcasted_iota(jnp.int32, seen_ref.shape, 0)
    offset = jnp.where(slot == 0, jnp.where(even, 1, 3), jnp.where(slot == 1, jnp.where(even, 3, 1), 2))
    seen_ref[...] = (offset <= shard - first).astype(jnp.int32)

    rows = own_ref[:lat, :].T
    for at in range(0, heads, GROUP):
        grads_ref[:, at * blk:(at + GROUP) * blk] = jnp.dot(
            rows, side_by_side(g_ref, at, GROUP), preferred_element_type=jnp.float32)


def own_grads(shard, doc_blocks, g, own):
    heads, lat, rows = g.shape
    return pl.pallas_call(
        own_kernel,
        in_specs=[SMEM] + [VMEM] * 3, out_specs=[VMEM, VMEM],
        out_shape=[
            jax.ShapeDtypeStruct((8, LANES), jnp.int32),
            jax.ShapeDtypeStruct((rows, heads * rows), jnp.float32),
        ],
        compiler_params=pltpu.CompilerParams(vmem_limit_bytes=30 * 1024 * 1024),
        cost_estimate=pl.CostEstimate(flops=OWN_FLOPS, bytes_accessed=0, transcendentals=0),
        name="own_grads",
    )(shard, doc_blocks, g, own)


def products_kernel(q_ref, g_ref, step_ref, own_ref, scores_ref, grads_ref):
    heads, lat, blk = g_ref.shape
    rows = jnp.concatenate([step_ref[...].T, own_ref[...].T], axis=0)
    for at in range(0, heads, GROUP):
        where = slice(at * blk, (at + GROUP) * blk)
        scores = jnp.dot(rows, side_by_side(q_ref, at, GROUP), preferred_element_type=jnp.float32)
        key = lax.broadcasted_iota(jnp.int32, scores[blk:].shape, 0)
        query = lax.broadcasted_iota(jnp.int32, scores[blk:].shape, 1) & (blk - 1)
        scores_ref[:blk, where] = scores[:blk]
        scores_ref[blk:, where] = jnp.where(key <= query, scores[blk:], -jnp.inf)
        grads_ref[:, where] = jnp.dot(
            rows[:blk, :lat], side_by_side(g_ref, at, GROUP), preferred_element_type=jnp.float32)


def products(q, g, step, own):
    heads, width, rows = q.shape
    return pl.pallas_call(
        products_kernel,
        in_specs=[VMEM] * 4, out_specs=[VMEM, VMEM],
        out_shape=[
            jax.ShapeDtypeStruct((2 * rows, heads * rows), jnp.float32),
            jax.ShapeDtypeStruct((rows, heads * rows), jnp.float32),
        ],
        compiler_params=pltpu.CompilerParams(vmem_limit_bytes=30 * 1024 * 1024),
        name="products",
    )(q, g, step, own)


def first_kernel(seen_ref, q_ref, g_ref, swap_ref, skip_ref, near_s, step_g, own_g,
                 swap_out, skip_out, step_out, own_out):
    heads, lat, blk = g_ref.shape
    rows = jnp.concatenate([swap_ref[...].T, skip_ref[...].T], axis=0)

    def products_of(at):
        q = side_by_side(q_ref, at, PART)
        g = side_by_side(g_ref, at, PART)
        scores = jnp.dot(rows, q, preferred_element_type=jnp.float32)
        grad_probs = jnp.dot(rows[:, :lat], g, preferred_element_type=jnp.float32)
        return at, q, g, scores, grad_probs

    def sums_of(at, q, g, scores, grad_probs):
        where = slice(at * blk, (at + PART) * blk)
        grad_probs = jnp.concatenate([grad_probs, step_g[:, where], own_g[:, where]], axis=0)
        parts = [scores[:blk], scores[blk:], near_s[:blk, where], near_s[blk:, where]]
        tops = [jnp.max(part, axis=0, keepdims=True) for part in parts]
        top = tops[3]
        for j in range(3):
            top = jnp.maximum(top, jnp.where(seen_ref[j:j + 1, :1] > 0, tops[j], -jnp.inf))
        top = top * to_exponent
        less = [jnp.where(seen_ref[j:j + 1, :1] > 0, top, jnp.inf) for j in range(3)] + [top]
        raised = jnp.concatenate([jnp.exp2(p * to_exponent - b) for p, b in zip(parts, less)], axis=0)
        inverse = 1.0 / jnp.sum(raised, axis=0, keepdims=True)
        dot = jnp.sum(raised * grad_probs, axis=0, keepdims=True) * inverse
        low = (raised * inverse).astype(jnp.bfloat16)
        grad_scores = ((raised * (inverse * softmax_scale)) * (grad_probs - dot)).astype(jnp.bfloat16)
        value = lax.dot_general(g, low, NT, preferred_element_type=jnp.float32)
        key = lax.dot_general(q, grad_scores, NT, preferred_element_type=jnp.float32)
        return value, key

    value = key = None
    after_this = products_of(0)
    for at in range(0, heads, PART):
        this = after_this
        if at + PART < heads:
            after_this = products_of(at + PART)
        more_value, more_key = sums_of(*this)
        value = more_value if value is None else value + more_value
        key = more_key if key is None else key + more_key
    for j, ref in enumerate((swap_out, skip_out, step_out, own_out)):
        mine = slice(j * blk, (j + 1) * blk)
        ref[:lat, :] = (key[:lat, mine] + value[:, mine]).astype(ref.dtype)
        ref[lat:, :] = key[lat:, mine].astype(ref.dtype)


def first_grads(seen, q, g, swap, skip, near_scores, step_grads, own_grads):
    heads, width, rows = q.shape
    sent = jax.ShapeDtypeStruct((width, rows), jnp.bfloat16)
    kept = jax.ShapeDtypeStruct((width, rows), jnp.float32)
    return pl.pallas_call(
        first_kernel,
        in_specs=[VMEM] * 8, out_specs=[VMEM] * 4, out_shape=[sent, sent, kept, kept],
        compiler_params=pltpu.CompilerParams(vmem_limit_bytes=30 * 1024 * 1024),
        name="first_grads",
    )(seen, q, g, swap, skip, near_scores, step_grads, own_grads)


def after(x, *others):
    return lax.optimization_barrier((x,) + others)[0]


def from_partner(x, n, shard):
    both = lax.all_gather(x, "ctx", axis_index_groups=[[i, i + 1] for i in range(0, n, 2)])
    return jnp.where(shard % 2 == 0, both[1], both[0])


def coded(x):
    largest = jnp.max(jnp.abs(x), axis=0, keepdims=True)
    power = jnp.ceil(jnp.log2(jnp.maximum(largest, 2.0 ** -100))) - HEADROOM
    values = (x * jnp.exp2(-power)).astype(jnp.float16)
    return jnp.concatenate([values, jnp.broadcast_to(power.astype(jnp.float16), (TILE,) + x.shape[1:])], axis=0)


def decoded(x):
    power = x[..., -TILE:-TILE + 1, :].astype(jnp.float32)
    return x[..., :-TILE, :].astype(jnp.float32) * jnp.exp2(power)


def coded_sum(x, pairs):
    return jnp.sum(decoded(lax.all_gather(coded(x), "head", axis_index_groups=pairs)), axis=0)


def plain_sum(x, pairs):
    both = lax.all_gather(x.astype(jnp.bfloat16), "head", axis_index_groups=pairs)
    return jnp.sum(both.astype(jnp.float32), axis=0)


def shards(queries, latent, out_grad, doc_blocks):
    n = lax.axis_size("ctx")
    shard = lax.axis_index("ctx")
    own = latent.T
    step = lax.ppermute(own, "ctx", step_pairs(n))
    skip = lax.ppermute(own, "ctx", skip_pairs(n))
    q = jnp.transpose(queries, (1, 2, 0))
    g = jnp.transpose(out_grad, (1, 2, 0))
    seen, of_own = own_grads(shard.reshape(1), doc_blocks.reshape(1, -1), g, own)
    step = after(step, of_own)
    swap = from_partner(step, n, shard)
    near_scores, of_step = products(q, g, step, own)
    swap, skip, step, near = first_grads(seen, q, g, swap, skip, near_scores, of_step, of_own)
    swap = from_partner(swap, n, shard)
    step = (step + swap.astype(jnp.float32)).astype(jnp.bfloat16)
    skip = after(skip, step)
    step = lax.ppermute(step, "ctx", turned(step_pairs(n)))
    skip = lax.ppermute(skip, "ctx", turned(skip_pairs(n)))
    near = near + step.astype(jnp.float32)
    near, skip = lax.optimization_barrier((near, skip))
    low = near + skip.astype(jnp.float32)
    return plain_sum(coded_sum(low, FIRST_PAIRS), SECOND_PAIRS).T


def solution(mesh):
    return jax.shard_map(
        shards,
        mesh=mesh,
        in_specs=(P("ctx", "head", None), P("ctx", None), P("ctx", "head", None), P()),
        out_specs=P("ctx", None),
        check_vma=False,
    )
```

```python
import math

import jax
import jax.numpy as jnp
from jax import lax
from jax.experimental import pallas as pl
from jax.experimental.pallas import tpu as pltpu
from jax.sharding import PartitionSpec as P

BLOCK = 128
GROUP = 8
PART = 4
TILE = 16
HEADROOM = 14
FIRST_PAIRS = [[0, 1], [2, 3]]
SECOND_PAIRS = [[0, 3], [1, 2]]
LANES = 128
OWN_FLOPS = 1 * 10 ** 9

softmax_scale = 192.0 ** (-0.5)
to_exponent = softmax_scale * math.log2(math.e)
NT = (((1,), (1,)), ((), ()))
VMEM = pl.BlockSpec(memory_space=pltpu.VMEM)
SMEM = pl.BlockSpec(memory_space=pltpu.SMEM)


def skip_pairs(n):
    ahead = [(i, i + 1 if i % 2 == 0 else i + 3) for i in range(n)]
    return [(i, j) for i, j in ahead if j < n]


def step_pairs(n):
    return [(i, i + 2) for i in range(n - 2)]


def swap_pairs(n):
    return [(i, i ^ 1) for i in range(n)]


def turned(pairs):
    return [(j, i) for i, j in pairs]


def side_by_side(ref, at, count):
    return jnp.concatenate([ref[at + h] for h in range(count)], axis=1)


def own_kernel(shard_ref, docs_ref, g_ref, own_ref, seen_ref, grads_ref):
    heads, lat, blk = g_ref.shape

    docs = docs_ref[...]
    square = (docs.shape[1], docs.shape[1])
    earlier = lax.broadcasted_iota(jnp.int32, square, 1) < lax.broadcasted_iota(jnp.int32, square, 0)
    starts = jnp.sum(jnp.where(earlier, docs, 0), axis=1, keepdims=True)
    shard = shard_ref[0]
    first = jnp.max(jnp.where(starts <= shard, starts, 0), axis=0, keepdims=True)
    even = lax.rem(shard, 2) == 0
    slot = lax.broadcasted_iota(jnp.int32, seen_ref.shape, 0)
    offset = jnp.where(slot == 0, jnp.where(even, 1, 3), jnp.where(slot == 1, jnp.where(even, 3, 1), 2))
    seen_ref[...] = (offset <= shard - first).astype(jnp.int32)

    rows = own_ref[:lat, :].T
    for at in range(0, heads, GROUP):
        grads_ref[:, at * blk:(at + GROUP) * blk] = jnp.dot(
            rows, side_by_side(g_ref, at, GROUP), preferred_element_type=jnp.float32)


def own_grads(shard, doc_blocks, g, own):
    heads, lat, rows = g.shape
    return pl.pallas_call(
        own_kernel,
        in_specs=[SMEM] + [VMEM] * 3, out_specs=[VMEM, VMEM],
        out_shape=[
            jax.ShapeDtypeStruct((8, LANES), jnp.int32),
            jax.ShapeDtypeStruct((rows, heads * rows), jnp.float32),
        ],
        compiler_params=pltpu.CompilerParams(vmem_limit_bytes=30 * 1024 * 1024),
        cost_estimate=pl.CostEstimate(flops=OWN_FLOPS, bytes_accessed=0, transcendentals=0),
        name="own_grads",
    )(shard, doc_blocks, g, own)


def first_kernel(seen_ref, q_ref, g_ref, swap_ref, skip_ref, step_ref, own_ref, own_g,
                 swap_out, skip_out, step_out, own_out):
    heads, lat, blk = g_ref.shape
    rows = jnp.concatenate([ref[...].T for ref in (swap_ref, skip_ref, step_ref, own_ref)], axis=0)
    cols = PART * blk
    late = (lax.broadcasted_iota(jnp.int32, (blk, cols), 0)
            > (lax.broadcasted_iota(jnp.int32, (blk, cols), 1) & (blk - 1)))

    def products_of(at):
        q = side_by_side(q_ref, at, PART)
        g = side_by_side(g_ref, at, PART)
        scores = jnp.dot(rows, q, preferred_element_type=jnp.float32)
        grad_probs = jnp.dot(rows[:3 * blk, :lat], g, preferred_element_type=jnp.float32)
        return at, q, g, scores, grad_probs

    def sums_of(at, q, g, scores, grad_probs):
        where = slice(at * blk, (at + PART) * blk)
        grad_probs = jnp.concatenate([grad_probs, own_g[:, where]], axis=0)
        parts = [scores[j * blk:(j + 1) * blk] for j in range(4)]
        parts[3] = jnp.where(late, -jnp.inf, parts[3])
        tops = [jnp.max(part, axis=0, keepdims=True) for part in parts]
        top = tops[3]
        for j in range(3):
            top = jnp.maximum(top, jnp.where(seen_ref[j:j + 1, :1] > 0, tops[j], -jnp.inf))
        top = top * to_exponent
        less = [jnp.where(seen_ref[j:j + 1, :1] > 0, top, jnp.inf) for j in range(3)] + [top]
        raised = jnp.concatenate([jnp.exp2(p * to_exponent - b) for p, b in zip(parts, less)], axis=0)
        inverse = 1.0 / jnp.sum(raised, axis=0, keepdims=True)
        dot = jnp.sum(raised * grad_probs, axis=0, keepdims=True) * inverse
        low = (raised * inverse).astype(jnp.bfloat16)
        grad_scores = ((raised * (inverse * softmax_scale)) * (grad_probs - dot)).astype(jnp.bfloat16)
        value = lax.dot_general(g, low, NT, preferred_element_type=jnp.float32)
        key = lax.dot_general(q, grad_scores, NT, preferred_element_type=jnp.float32)
        return value, key

    value = key = None
    after_this = products_of(0)
    for at in range(0, heads, PART):
        this = after_this
        if at + PART < heads:
            after_this = products_of(at + PART)
        more_value, more_key = sums_of(*this)
        value = more_value if value is None else value + more_value
        key = more_key if key is None else key + more_key
    for j, ref in enumerate((swap_out, skip_out, step_out, own_out)):
        mine = slice(j * blk, (j + 1) * blk)
        ref[:lat, :] = (key[:lat, mine] + value[:, mine]).astype(ref.dtype)
        ref[lat:, :] = key[lat:, mine].astype(ref.dtype)


def first_grads(seen, q, g, swap, skip, step, own, own_grads):
    heads, width, rows = q.shape
    sent = jax.ShapeDtypeStruct((width, rows), jnp.bfloat16)
    kept = jax.ShapeDtypeStruct((width, rows), jnp.float32)
    return pl.pallas_call(
        first_kernel,
        in_specs=[VMEM] * 8, out_specs=[VMEM] * 4, out_shape=[sent, sent, kept, kept],
        compiler_params=pltpu.CompilerParams(vmem_limit_bytes=30 * 1024 * 1024),
        name="first_grads",
    )(seen, q, g, swap, skip, step, own, own_grads)


def after(x, *others):
    return lax.optimization_barrier((x,) + others)[0]


def from_partner(x, n, shard):
    both = lax.all_gather(x, "ctx", axis_index_groups=[[i, i + 1] for i in range(0, n, 2)])
    return jnp.where(shard % 2 == 0, both[1], both[0])


def coded(x):
    largest = jnp.max(jnp.abs(x), axis=0, keepdims=True)
    power = jnp.ceil(jnp.log2(jnp.maximum(largest, 2.0 ** -100))) - HEADROOM
    values = (x * jnp.exp2(-power)).astype(jnp.float16)
    return jnp.concatenate([values, jnp.broadcast_to(power.astype(jnp.float16), (TILE,) + x.shape[1:])], axis=0)


def decoded(x):
    power = x[..., -TILE:-TILE + 1, :].astype(jnp.float32)
    return x[..., :-TILE, :].astype(jnp.float32) * jnp.exp2(power)


def coded_sum(x, pairs):
    return jnp.sum(decoded(lax.all_gather(coded(x), "head", axis_index_groups=pairs)), axis=0)


def plain_sum(x, pairs):
    both = lax.all_gather(x.astype(jnp.bfloat16), "head", axis_index_groups=pairs)
    return jnp.sum(both.astype(jnp.float32), axis=0)


def shards(queries, latent, out_grad, doc_blocks):
    n = lax.axis_size("ctx")
    shard = lax.axis_index("ctx")
    own = latent.T
    step = lax.ppermute(own, "ctx", step_pairs(n))
    skip = lax.ppermute(own, "ctx", skip_pairs(n))
    q = jnp.transpose(queries, (1, 2, 0))
    g = jnp.transpose(out_grad, (1, 2, 0))
    seen, of_own = own_grads(shard.reshape(1), doc_blocks.reshape(1, -1), g, own)
    step = after(step, of_own)
    swap = from_partner(step, n, shard)
    swap, skip, step, near = first_grads(seen, q, g, swap, skip, step, own, of_own)
    swap = from_partner(swap, n, shard)
    step = (step + swap.astype(jnp.float32)).astype(jnp.bfloat16)
    skip = after(skip, step)
    step = lax.ppermute(step, "ctx", turned(step_pairs(n)))
    skip = lax.ppermute(skip, "ctx", turned(skip_pairs(n)))
    near = near + step.astype(jnp.float32)
    near, skip = lax.optimization_barrier((near, skip))
    low = near + skip.astype(jnp.float32)
    return plain_sum(coded_sum(low, FIRST_PAIRS), SECOND_PAIRS).T


def solution(mesh):
    return jax.shard_map(
        shards,
        mesh=mesh,
        in_specs=(P("ctx", "head", None), P("ctx", None), P("ctx", "head", None), P()),
        out_specs=P("ctx", None),
        check_vma=False,
    )
```

```python
import math

import jax
import jax.numpy as jnp
from jax import lax
from jax.experimental import pallas as pl
from jax.experimental.pallas import tpu as pltpu
from jax.sharding import PartitionSpec as P

BLOCK = 128
GROUP = 8
PART = 4
TILE = 16
HEADROOM = 14
FIRST_PAIRS = [[0, 1], [2, 3]]
SECOND_PAIRS = [[0, 3], [1, 2]]
LANES = 128
OWN_FLOPS = 1 * 10 ** 9

softmax_scale = 192.0 ** (-0.5)
to_exponent = softmax_scale * math.log2(math.e)
NT = (((1,), (1,)), ((), ()))
VMEM = pl.BlockSpec(memory_space=pltpu.VMEM)
SMEM = pl.BlockSpec(memory_space=pltpu.SMEM)


def skip_pairs(n):
    ahead = [(i, i + 1 if i % 2 == 0 else i + 3) for i in range(n)]
    return [(i, j) for i, j in ahead if j < n]


def step_pairs(n):
    return [(i, i + 2) for i in range(n - 2)]


def swap_pairs(n):
    return [(i, i ^ 1) for i in range(n)]


def turned(pairs):
    return [(j, i) for i, j in pairs]


def side_by_side(ref, at, count):
    return jnp.concatenate([ref[at + h] for h in range(count)], axis=1)


def own_kernel(shard_ref, docs_ref, g_ref, own_ref, seen_ref, grads_ref):
    heads, lat, blk = g_ref.shape

    docs = docs_ref[...]
    square = (docs.shape[1], docs.shape[1])
    earlier = lax.broadcasted_iota(jnp.int32, square, 1) < lax.broadcasted_iota(jnp.int32, square, 0)
    starts = jnp.sum(jnp.where(earlier, docs, 0), axis=1, keepdims=True)
    shard = shard_ref[0]
    first = jnp.max(jnp.where(starts <= shard, starts, 0), axis=0, keepdims=True)
    even = lax.rem(shard, 2) == 0
    slot = lax.broadcasted_iota(jnp.int32, seen_ref.shape, 0)
    offset = jnp.where(slot == 0, jnp.where(even, 1, 3), jnp.where(slot == 1, jnp.where(even, 3, 1), 2))
    seen_ref[...] = (offset <= shard - first).astype(jnp.int32)

    rows = own_ref[:lat, :].T
    for at in range(0, heads, GROUP):
        grads_ref[:, at * blk:(at + GROUP) * blk] = jnp.dot(
            rows, side_by_side(g_ref, at, GROUP), preferred_element_type=jnp.float32)


def own_grads(shard, doc_blocks, g, own):
    heads, lat, rows = g.shape
    return pl.pallas_call(
        own_kernel,
        in_specs=[SMEM] + [VMEM] * 3, out_specs=[VMEM, VMEM],
        out_shape=[
            jax.ShapeDtypeStruct((8, LANES), jnp.int32),
            jax.ShapeDtypeStruct((rows, heads * rows), jnp.float32),
        ],
        compiler_params=pltpu.CompilerParams(vmem_limit_bytes=30 * 1024 * 1024),
        cost_estimate=pl.CostEstimate(flops=OWN_FLOPS, bytes_accessed=0, transcendentals=0),
        name="own_grads",
    )(shard, doc_blocks, g, own)


def first_kernel(seen_ref, q_ref, g_ref, swap_ref, skip_ref, step_ref, own_ref, own_g,
                 swap_out, skip_out, step_out, own_out):
    heads, lat, blk = g_ref.shape
    rows = jnp.concatenate([ref[...].T for ref in (swap_ref, skip_ref, step_ref, own_ref)], axis=0)
    cols = PART * blk
    late = (lax.broadcasted_iota(jnp.int32, (blk, cols), 0)
            > (lax.broadcasted_iota(jnp.int32, (blk, cols), 1) & (blk - 1)))

    def products_of(at):
        q = side_by_side(q_ref, at, PART)
        g = side_by_side(g_ref, at, PART)
        scores = jnp.dot(rows, q, preferred_element_type=jnp.float32)
        grad_probs = jnp.dot(rows[:3 * blk, :lat], g, preferred_element_type=jnp.float32)
        return at, q, g, scores, grad_probs

    def sums_of(at, q, g, scores, grad_probs):
        where = slice(at * blk, (at + PART) * blk)
        grad_probs = jnp.concatenate([grad_probs, own_g[:, where]], axis=0)
        parts = [scores[j * blk:(j + 1) * blk] for j in range(4)]
        parts[3] = jnp.where(late, -jnp.inf, parts[3])
        tops = [jnp.max(part, axis=0, keepdims=True) for part in parts]
        top = tops[3]
        for j in range(3):
            top = jnp.maximum(top, jnp.where(seen_ref[j:j + 1, :1] > 0, tops[j], -jnp.inf))
        top = top * to_exponent
        less = [jnp.where(seen_ref[j:j + 1, :1] > 0, top, jnp.inf) for j in range(3)] + [top]
        raised = jnp.concatenate([jnp.exp2(p * to_exponent - b) for p, b in zip(parts, less)], axis=0)
        inverse = 1.0 / jnp.sum(raised, axis=0, keepdims=True)
        dot = jnp.sum(raised * grad_probs, axis=0, keepdims=True) * inverse
        low = (raised * inverse).astype(jnp.bfloat16)
        grad_scores = ((raised * (inverse * softmax_scale)) * (grad_probs - dot)).astype(jnp.bfloat16)
        halves = [slice(0, 2 * blk), slice(2 * blk, 4 * blk)]
        value = [lax.dot_general(g, low[half], NT, preferred_element_type=jnp.float32) for half in halves]
        key = [lax.dot_general(q, grad_scores[half], NT, preferred_element_type=jnp.float32) for half in halves]
        return jnp.concatenate(value, axis=1), jnp.concatenate(key, axis=1)

    value = key = None
    after_this = products_of(0)
    for at in range(0, heads, PART):
        this = after_this
        if at + PART < heads:
            after_this = products_of(at + PART)
        more_value, more_key = sums_of(*this)
        value = more_value if value is None else value + more_value
        key = more_key if key is None else key + more_key
    for j, ref in enumerate((swap_out, skip_out, step_out, own_out)):
        mine = slice(j * blk, (j + 1) * blk)
        ref[:lat, :] = (key[:lat, mine] + value[:, mine]).astype(ref.dtype)
        ref[lat:, :] = key[lat:, mine].astype(ref.dtype)


def first_grads(seen, q, g, swap, skip, step, own, own_grads):
    heads, width, rows = q.shape
    sent = jax.ShapeDtypeStruct((width, rows), jnp.bfloat16)
    kept = jax.ShapeDtypeStruct((width, rows), jnp.float32)
    return pl.pallas_call(
        first_kernel,
        in_specs=[VMEM] * 8, out_specs=[VMEM] * 4, out_shape=[sent, sent, kept, kept],
        compiler_params=pltpu.CompilerParams(vmem_limit_bytes=30 * 1024 * 1024),
        name="first_grads",
    )(seen, q, g, swap, skip, step, own, own_grads)


def after(x, *others):
    return lax.optimization_barrier((x,) + others)[0]


def from_partner(x, n, shard):
    both = lax.all_gather(x, "ctx", axis_index_groups=[[i, i + 1] for i in range(0, n, 2)])
    return jnp.where(shard % 2 == 0, both[1], both[0])


def coded(x):
    largest = jnp.max(jnp.abs(x), axis=0, keepdims=True)
    power = jnp.ceil(jnp.log2(jnp.maximum(largest, 2.0 ** -100))) - HEADROOM
    values = (x * jnp.exp2(-power)).astype(jnp.float16)
    return jnp.concatenate([values, jnp.broadcast_to(power.astype(jnp.float16), (TILE,) + x.shape[1:])], axis=0)


def decoded(x):
    power = x[..., -TILE:-TILE + 1, :].astype(jnp.float32)
    return x[..., :-TILE, :].astype(jnp.float32) * jnp.exp2(power)


def coded_sum(x, pairs):
    return jnp.sum(decoded(lax.all_gather(coded(x), "head", axis_index_groups=pairs)), axis=0)


def plain_sum(x, pairs):
    both = lax.all_gather(x.astype(jnp.bfloat16), "head", axis_index_groups=pairs)
    return jnp.sum(both.astype(jnp.float32), axis=0)


def shards(queries, latent, out_grad, doc_blocks):
    n = lax.axis_size("ctx")
    shard = lax.axis_index("ctx")
    own = latent.T
    step = lax.ppermute(own, "ctx", step_pairs(n))
    skip = lax.ppermute(own, "ctx", skip_pairs(n))
    q = jnp.transpose(queries, (1, 2, 0))
    g = jnp.transpose(out_grad, (1, 2, 0))
    seen, of_own = own_grads(shard.reshape(1), doc_blocks.reshape(1, -1), g, own)
    step = after(step, of_own)
    swap = from_partner(step, n, shard)
    swap, skip, step, near = first_grads(seen, q, g, swap, skip, step, own, of_own)
    swap = from_partner(swap, n, shard)
    step = (step + swap.astype(jnp.float32)).astype(jnp.bfloat16)
    skip = after(skip, step)
    step = lax.ppermute(step, "ctx", turned(step_pairs(n)))
    skip = lax.ppermute(skip, "ctx", turned(skip_pairs(n)))
    near = near + step.astype(jnp.float32)
    near, skip = lax.optimization_barrier((near, skip))
    low = near + skip.astype(jnp.float32)
    return plain_sum(coded_sum(low, FIRST_PAIRS), SECOND_PAIRS).T


def solution(mesh):
    return jax.shard_map(
        shards,
        mesh=mesh,
        in_specs=(P("ctx", "head", None), P("ctx", None), P("ctx", "head", None), P()),
        out_specs=P("ctx", None),
        check_vma=False,
    )
```
